32 devices in a mesh: groups: 2 (over x), aux: 16 (over z, y, core).
Axes of the slice: x: 2, y: 2, z: 4, core: 2. Of those that a mesh axis runs over, the one named last changes fastest.
Arguments:
- b_factors: bfloat16 [32, 850, 4096], P('groups', None, 'aux'), parts along dimension 0, may hold values from -0.75 to 0.75
- occ_energy: float32 [32], P('groups'), parts along dimension 0, may hold values from -1.2 to -0.4
- vir_energy: float32 [1700], P('groups'), parts along dimension 0, may hold values from 0.2 to 2.5
- kept: int32 [32], P('groups'), parts along dimension 0, may hold values 0 or 1
Outputs:
- gamma: bfloat16 [32, 850, 4096], P('groups', None, 'aux'), parts along dimension 0
The draws below stay inside these ranges and needn't reach their ends.
There are 2 independent parts, one for each index of `groups`. The reference program is written for one: setup_inputs(seed, part) draws one part's arguments, and reference() takes and returns one part's arrays. A program takes and returns all parts, laid end to end along the dimension named above; each array names one. Nothing has to cross between parts.
Inputs may be any that keep to these rules, and one draw needn't show every extreme that they name: kept[i] = 1 keeps the pair of orbitals i and i + 1 modulo 16.
All inputs are finite; a program needn't handle non-finite values.
Results may differ from the reference program's by a relative error of at most 0.0045.
Values may be sent and summed in bfloat16 or wider, within the bound.
A program may use at most 192 MiB of HBM per device.

```python
import jax
import jax.numpy as jnp
from jax import lax

NV = 850
NAUX = 4096
OCC = 16


def with_ends(values, stream_key, least, top_value):
    extent = values.shape
    place = [jax.random.randint(jax.random.fold_in(stream_key, axis), (), 0, extent[axis]) for axis in range(len(extent))]
    values = values.at[tuple(place)].set(least)
    longest = extent.index(max(extent))
    place[longest] = (place[longest] + 1) % extent[longest]
    return values.at[tuple(place)].set(top_value)


def steps_of(own_key, shape, pieces, low, high):
    loudness, own = 1.0, jax.random.fold_in(own_key, 6)
    for dim, blocks in pieces:
        heights = jnp.exp(jax.random.uniform(jax.random.fold_in(own, dim), (blocks,), jnp.float32, low / len(pieces), high / len(pieces)))
        loudness = loudness * jnp.repeat(heights, shape[dim] // blocks).reshape([-1 if axis == dim else 1 for axis in range(len(shape))])
    return loudness


def bell_draw(rng, extent, deviation, bound, shards=(), kind=jnp.bfloat16):
    entries = deviation * jax.random.normal(rng, extent, jnp.float32)
    if shards:
        entries = entries * steps_of(rng, extent, shards, -0.22, 0.18)
    return jnp.clip(entries, -bound, bound).astype(kind)


def setup_inputs(seed: int = 0, part: int = 0) -> dict:
    splits = jax.random.split(jax.random.key(seed), 5)
    own_keys = jax.random.split(jax.random.fold_in(splits[4], part), 5)
    b_factors = bell_draw(own_keys[0], (OCC, NV, NAUX), (NAUX ** 0.5) ** -0.5, 0.75, ((2, 16),))
    occ_energy = jnp.clip(jax.random.uniform(own_keys[1], (OCC,), jnp.float32, -1.2, -0.4), -1.2, -0.4)
    vir_energy = jnp.clip(jax.random.uniform(own_keys[2], (NV,), jnp.float32, 0.2, 2.5), 0.2, 2.5)
    kept = with_ends((jax.random.randint(own_keys[3], (OCC,), 0, 2) < 1).astype(jnp.int32), jax.random.fold_in(own_keys[3], 1), 0, 1)
    return dict(b_factors=b_factors, occ_energy=occ_energy, vir_energy=vir_energy, kept=kept)


def amplitudes(left, right, e_left, e_right, vir_energy):
    coulomb = lax.dot_general(left, right, (((1,), (1,)), ((), ())), preferred_element_type=jnp.float32)
    denom = e_left + e_right - vir_energy[:, None] - vir_energy[None, :]
    t_pair = coulomb / denom
    return (2.0 * t_pair - t_pair.T).astype(jnp.bfloat16)


def reference(b_factors, occ_energy, vir_energy, kept):
    following = jnp.roll(b_factors, -1, axis=0)
    e_next = jnp.roll(occ_energy, -1)

    def single(items):
        own, after, e_own, e_after, flag = items
        u_own = amplitudes(own, own, e_own, e_own, vir_energy)
        diag = jnp.dot(u_own, own, preferred_element_type=jnp.float32)

        def with_pair(unused):
            u_pair = amplitudes(own, after, e_own, e_after, vir_energy)
            mine = jnp.dot(u_pair, after, preferred_element_type=jnp.float32)
            theirs = lax.dot_general(u_pair, own, (((0,), (0,)), ((), ())), preferred_element_type=jnp.float32)
            return mine, theirs

        def without(unused):
            zeros = jnp.zeros(own.shape, jnp.float32)
            return zeros, zeros

        mine, theirs = lax.cond(flag == 1, with_pair, without, 0)
        return diag + mine, theirs

    selfs, theirs = lax.map(single, (b_factors, following, occ_energy, e_next, kept))
    gamma = selfs + jnp.roll(theirs, 1, axis=0)
    return gamma.astype(jnp.bfloat16)
```

```python
import jax
import jax.numpy as jnp
from jax import lax
from jax.sharding import PartitionSpec as P


def passed_along(block, axis, distance):
    devices = range(lax.axis_size(axis))
    route = [((i - distance) % len(devices), i) for i in devices]
    return lax.ppermute(block, axis, route)


def amplitudes(left, right, e_left, e_right, vir_energy):
    coulomb = lax.dot_general(
        left, right, (((1,), (1,)), ((), ())), preferred_element_type=jnp.float32
    )
    denom = e_left + e_right - vir_energy[:, None] - vir_energy[None, :]
    t_pair = coulomb / denom
    return (2.0 * t_pair - t_pair.T).astype(jnp.bfloat16)


def body(b_factors, occ_energy, vir_energy, kept):
    owned = lax.all_to_all(b_factors, "aux", split_axis=0, concat_axis=2, tiled=True)[0]
    index = lax.axis_index("aux")
    count = lax.axis_size("aux")
    later = (index + 1) % count
    e_own = lax.dynamic_index_in_dim(occ_energy, index, 0, False)
    e_after = lax.dynamic_index_in_dim(occ_energy, later, 0, False)
    flag = lax.dynamic_index_in_dim(kept, index, 0, False)
    after = passed_along(owned, "aux", -1)
    u_own = amplitudes(owned, owned, e_own, e_own, vir_energy)
    diag = jnp.dot(u_own, owned, preferred_element_type=jnp.float32)
    zeros = jnp.zeros(owned.shape, jnp.bfloat16)

    def with_pair(unused):
        u_pair = amplitudes(owned, after, e_own, e_after, vir_energy)
        mine = jnp.dot(u_pair, after, preferred_element_type=jnp.float32)
        theirs = lax.dot_general(
            u_pair, owned, (((0,), (0,)), ((), ())), preferred_element_type=jnp.float32
        )
        return (mine.astype(jnp.bfloat16), theirs.astype(jnp.bfloat16))

    def without(unused):
        return (zeros, zeros)

    mine, theirs = lax.cond(flag == 1, with_pair, without, 0)
    mine = mine.astype(jnp.float32)
    incoming = passed_along(theirs, "aux", 1).astype(jnp.float32)
    gamma = (diag + mine + incoming).astype(jnp.bfloat16)
    sliced = gamma.reshape(gamma.shape[0], count, -1).transpose(1, 0, 2)
    return lax.all_to_all(sliced, "aux", split_axis=0, concat_axis=0, tiled=True)


def solution(mesh):
    placed = (P("groups", None, "aux"), P("groups"), P("groups"), P("groups"))
    return jax.shard_map(
        body, mesh=mesh, in_specs=placed, out_specs=P("groups", None, "aux"), check_vma=False
    )
```

```python
import functools

import jax
import jax.numpy as jnp
from jax import lax
from jax.experimental import pallas as pl
from jax.experimental.pallas import tpu as pltpu
from jax.sharding import PartitionSpec as P

PLANES = 4
STRIP = 256
MESH = pl.DeviceIdType.MESH
F32, BF16 = jnp.float32, jnp.bfloat16


def up_to(size, unit):
    return -(-size // unit) * unit


def kernel(
    m, k, occ_ref, kept_ref, vrow_ref, vcol_ref, x_ref, out_ref,
    bs, cbuf, rbuf, xbuf, tt, gbuf,
    b_send, b_recv, b_local, s12, s3, r13, r2, t_send, t_recv, g_send, g_recv, g_local,
):
    occ, nvp, qd = x_ref.shape
    nvr = out_ref.shape[1]
    me = lax.axis_index("aux")
    plane, q = me // m, me % m
    first = plane * m
    outer = (plane == 0) | (plane == PLANES - 1)
    side = plane // 2
    hop_plane = jnp.where(outer, 1 + side, 3 * side)
    hop = {"aux": hop_plane * m + q}
    across = {"aux": (3 - plane) * m + q}
    strips = [(a, min(a + STRIP, nvp)) for a in range(0, nvp, STRIP)]

    barrier = pltpu.get_barrier_semaphore()
    for d in range(1, m):
        peer = first + (q + d) % m
        pl.semaphore_signal(barrier, inc=1, device_id={"aux": peer}, device_id_type=MESH)
    pl.semaphore_signal(barrier, inc=1, device_id=hop, device_id_type=MESH)

    @pl.when(jnp.logical_not(outer))
    def _():
        pl.semaphore_signal(barrier, inc=1, device_id=across, device_id_type=MESH)
        pl.semaphore_wait(barrier, m + 1)

    @pl.when(outer)
    def _():
        pl.semaphore_wait(barrier, m)

    def lanes(p):
        return pl.ds(pl.multiple_of(p * qd, qd), qd)

    def b_copy(slot, d):
        p = (q + d) % m
        return pltpu.make_async_remote_copy(
            src_ref=x_ref.at[(k * p + slot) % occ], dst_ref=bs.at[slot, :, lanes(q)],
            send_sem=b_send.at[slot, d - 1], recv_sem=b_recv.at[slot, d - 1],
            device_id={"aux": first + p}, device_id_type=MESH,
        )

    def b_own(slot):
        return pltpu.make_async_copy(
            x_ref.at[(k * q + slot) % occ], bs.at[slot, :, lanes(q)], b_local.at[slot]
        )

    def b_wait(slot):
        b_own(slot).wait()
        for d in range(1, m):
            p = (q + m - d) % m
            pltpu.make_async_remote_copy(
                src_ref=x_ref.at[0], dst_ref=bs.at[slot, :, lanes(p)],
                send_sem=b_send.at[slot, d - 1], recv_sem=b_recv.at[slot, d - 1],
                device_id={"aux": first + p}, device_id_type=MESH,
            ).wait_recv()

    @pl.loop(0, k + 1)
    def _(i):
        slot = jnp.where(i < 2, k - 1 + i, i - 2)
        b_own(slot).start()
        for d in range(1, m):
            b_copy(slot, d).start()

    def piece(buf, unit, kind, c):
        a, b = strips[c]
        return buf.at[unit, a:b, (0 if kind else a) : nvp]

    def hop_copy(src, dst, send, recv, target, unit, kind, c):
        return pltpu.make_async_remote_copy(
            src_ref=piece(src, unit, kind, c), dst_ref=piece(dst, unit, kind, c),
            send_sem=send.at[unit, c], recv_sem=recv.at[unit, c],
            device_id=target, device_id_type=MESH,
        )

    def inward(unit, kind, c):
        return hop_copy(cbuf, rbuf, s12, r13, hop, unit, kind, c)

    def exchange(unit, kind, c):
        return hop_copy(cbuf, xbuf, s12, r2, across, unit, kind, c)

    def outward(unit, kind, c):
        return hop_copy(rbuf, rbuf, s3, r13, hop, unit, kind, c)

    def partial(r, kind):
        s = (r + k - 1) % k
        unit = 2 * r + kind
        for c, (a, b) in enumerate(strips):
            low = 0 if kind else a
            got = lax.dot_general(
                bs[s, a:b, :], bs[s + kind, low:nvp, :], (((1,), (1,)), ((), ())),
                preferred_element_type=F32,
            )
            piece(cbuf, unit, kind, c)[...] = got.astype(BF16)

            @pl.when(outer)
            def _():
                inward(unit, kind, c).start()

        @pl.when(jnp.logical_not(outer))
        def _():
            for c in range(len(strips)):
                inward(unit, kind, c).wait_recv()
                mine, theirs = piece(cbuf, unit, kind, c), piece(rbuf, unit, kind, c)
                mine[...] = (mine[...].astype(F32) + theirs[...].astype(F32)).astype(BF16)
                exchange(unit, kind, c).start()

    def energies(r, kind):
        s = (r + k - 1) % k
        i = (k * q + s) % occ
        j = (i + kind) % occ
        return occ_ref[i] + occ_ref[j], kept_ref[i] == 1

    def t_block(unit, e, a, b, c, d):
        coulomb = cbuf[unit, a:b, c:d].astype(F32) + xbuf[unit, a:b, c:d].astype(F32)
        return coulomb / (e - vcol_ref[a:b, :] - vrow_ref[:, c:d])

    def u_diag(r):
        unit = 2 * r
        e, _ = energies(r, 0)
        for c, (a, b) in enumerate(strips):
            exchange(unit, 0, c).wait_recv()
            rbuf[unit, a:b, a:nvp] = t_block(unit, e, a, b, a, nvp).astype(BF16)
            outward(unit, 0, c).start()

    def u_pair(r):
        unit = 2 * r + 1
        e, flag = energies(r, 1)
        for c in range(len(strips)):
            exchange(unit, 1, c).wait_recv()
        for c, (a, b) in enumerate(strips):
            for a2, b2 in strips[c:]:
                upper = t_block(unit, e, a, b, a2, b2)
                lower = upper if a2 == a else t_block(unit, e, a2, b2, a, b)
                u = jnp.where(flag, 2.0 * upper - lower.T, 0.0)
                rbuf[unit, a:b, a2:b2] = u.astype(BF16)
                if a2 != a:
                    u = jnp.where(flag, 2.0 * lower - upper.T, 0.0)
                    rbuf[unit, a2:b2, a:b] = u.astype(BF16)
            outward(unit, 1, c).start()

    def t_copy():
        return pltpu.make_async_remote_copy(
            src_ref=tt.at[0], dst_ref=tt.at[1], send_sem=t_send, recv_sem=t_recv,
            device_id={"aux": first + (q + 1) % m}, device_id_type=MESH,
        )

    def g_copy(s, d):
        p = (q + d) % m
        return pltpu.make_async_remote_copy(
            src_ref=gbuf.at[s, 0:nvr, lanes(p)], dst_ref=out_ref.at[k * q + s, 0:nvr, :],
            send_sem=g_send.at[s, d - 1], recv_sem=g_recv.at[s, d - 1],
            device_id={"aux": first + p}, device_id_type=MESH,
        )

    def g_own(s):
        return pltpu.make_async_copy(
            gbuf.at[s, 0:nvr, lanes(q)], out_ref.at[k * q + s, 0:nvr, :], g_local.at[s]
        )

    def density(r):
        s = (r + k - 1) % k
        diag = 2 * (r % k)

        @pl.when(r < k)
        def _():
            @pl.when(outer)
            def _():
                for kind in (0, 1):
                    for c in range(len(strips)):
                        outward(2 * r + kind, kind, c).wait_recv()

            for c, (a, b) in enumerate(strips):
                for a2, b2 in strips[c + 1 :]:
                    mirrored = rbuf[diag, a:b, a2:b2].astype(F32).T
                    rbuf[diag, a2:b2, a:b] = mirrored.astype(BF16)

        @pl.when(r == 1)
        def _():
            t_copy().wait_recv()

        @pl.when(r >= 1)
        def _():
            for a, b in strips:
                total = jnp.dot(rbuf[diag, a:b, :], bs[s], preferred_element_type=F32)
                total += jnp.dot(rbuf[diag + 1, a:b, :], bs[s + 1], preferred_element_type=F32)
                gbuf[s, a:b, :] = (total + tt[1, a:b, :].astype(F32)).astype(BF16)
            g_own(s).start()
            for d in range(1, m):
                g_copy(s, d).start()

        @pl.when(r < k)
        def _():
            where = jnp.where(r == 0, 0, 1)
            for a, b in strips:
                got = lax.dot_general(
                    rbuf[diag + 1, :, a:b], bs[s], (((0,), (0,)), ((), ())),
                    preferred_element_type=F32,
                )
                tt[where, a:b, :] = got.astype(BF16)

        @pl.when(r == 0)
        def _():
            t_copy().start()

    @pl.loop(0, k + 2)
    def _(r):
        s = (r + k - 1) % k

        @pl.when(r <= 1)
        def _():
            b_wait(s)

        @pl.when(r < k)
        def _():
            partial(r, 0)

        @pl.when((r >= 1) & (r <= k) & jnp.logical_not(outer))
        def _():
            u_pair(r - 1)

        @pl.when(r < k - 1)
        def _():
            b_wait(s + 1)

        @pl.when(r < k)
        def _():
            partial(r, 1)

        @pl.when((r < k) & jnp.logical_not(outer))
        def _():
            u_diag(r)

        @pl.when(r >= 1)
        def _():
            density(r - 1)

    t_copy().wait_send()

    @pl.loop(0, k + 1)
    def _(slot):
        for d in range(1, m):
            b_copy(slot, d).wait_send()

    @pl.loop(0, k)
    def _(s):
        for kind in (0, 1):
            for c in range(len(strips)):
                inward(2 * s + kind, kind, c).wait_send()

        @pl.when(jnp.logical_not(outer))
        def _():
            for kind in (0, 1):
                for c in range(len(strips)):
                    outward(2 * s + kind, kind, c).wait_send()

        g_own(s).wait()
        for d in range(1, m):
            g_copy(s, d).wait_send()
            p = (q + m - d) % m
            pltpu.make_async_remote_copy(
                src_ref=gbuf.at[s, 0:nvr, lanes(p)], dst_ref=out_ref.at[k * p + s, 0:nvr, :],
                send_sem=g_send.at[s, d - 1], recv_sem=g_recv.at[s, d - 1],
                device_id={"aux": first + p}, device_id_type=MESH,
            ).wait_recv()


def body(b_factors, occ_energy, vir_energy, kept):
    occ, nv, qd = b_factors.shape
    m = lax.axis_size("aux") // PLANES
    k = occ // m
    nvp, nvr = up_to(nv, 128), up_to(nv, 16)
    x = jnp.pad(b_factors, ((0, 0), (0, nvp - nv), (0, 0)))
    vir = jnp.pad(vir_energy, (0, nvp - nv), constant_values=1.0)
    pieces = len(range(0, nvp, STRIP))
    square = pltpu.VMEM((2 * k, nvp, nvp), BF16)
    dma = pltpu.SemaphoreType.DMA
    flops = 2 * nvp * nvp * m * qd * 5 * k
    out = pl.pallas_call(
        functools.partial(kernel, m, k),
        out_shape=jax.ShapeDtypeStruct((occ, nvr, qd), BF16),
        in_specs=[pl.BlockSpec(memory_space=pltpu.SMEM)] * 2
        + [pl.BlockSpec(memory_space=pltpu.VMEM)] * 2
        + [pl.BlockSpec(memory_space=pl.ANY)],
        out_specs=pl.BlockSpec(memory_space=pl.ANY),
        scratch_shapes=[
            pltpu.VMEM((k + 1, nvp, m * qd), BF16), square, square, square,
            pltpu.VMEM((2, nvp, m * qd), BF16), pltpu.VMEM((k, nvp, m * qd), BF16),
            dma((k + 1, m - 1)), dma((k + 1, m - 1)), dma((k + 1,)),
            dma((2 * k, pieces)), dma((2 * k, pieces)), dma((2 * k, pieces)), dma((2 * k, pieces)),
            dma, dma, dma((k, m - 1)), dma((k, m - 1)), dma((k,)),
        ],
        compiler_params=pltpu.CompilerParams(
            collective_id=0, has_side_effects=True, vmem_limit_bytes=63 * 2**20
        ),
        cost_estimate=pl.CostEstimate(flops=flops, bytes_accessed=4 * x.size, transcendentals=0),
    )(occ_energy, kept, vir[None, :], vir[:, None], x)
    return out[:, :nv]


def solution(mesh):
    placed = (P("groups", None, "aux"), P("groups"), P("groups"), P("groups"))
    return jax.shard_map(
        body, mesh=mesh, in_specs=placed, out_specs=P("groups", None, "aux"), check_vma=False
    )
```

```python
import functools

import jax
import jax.numpy as jnp
from jax import lax
from jax.experimental import pallas as pl
from jax.experimental.pallas import tpu as pltpu
from jax.sharding import PartitionSpec as P

PLANES = 4
STRIP, WIDE = 128, 256
MESH = pl.DeviceIdType.MESH
F32, BF16 = jnp.float32, jnp.bfloat16


def up_to(size, unit):
    return -(-size // unit) * unit


def kernel(
    m, k, occ_ref, kept_ref, vrow_ref, vcol_ref, x_ref, out_ref,
    bs, cbuf, rbuf, xbuf, tt, gbuf,
    b_send, b_recv, b_local, s12, s3, r13, r2, t_send, t_recv, g_send, g_recv, g_local,
):
    occ, nvp, qd = x_ref.shape
    nvr = out_ref.shape[1]
    me = lax.axis_index("aux")
    plane, q = me // m, me % m
    first = plane * m
    outer = (plane == 0) | (plane == PLANES - 1)
    side = plane // 2
    hop_plane = jnp.where(outer, 1 + side, 3 * side)
    hop = {"aux": hop_plane * m + q}
    across = {"aux": (3 - plane) * m + q}
    strips = [(a, a + STRIP) for a in range(0, nvp, STRIP)]
    wide = [(a, min(a + WIDE, nvp)) for a in range(0, nvp, WIDE)]

    for unit in range(1, 2 * k, 2):
        xbuf[unit, nvr:nvp, :] = jnp.zeros((nvp - nvr, nvp), BF16)

    barrier = pltpu.get_barrier_semaphore()
    for d in range(1, m):
        peer = first + (q + d) % m
        pl.semaphore_signal(barrier, inc=1, device_id={"aux": peer}, device_id_type=MESH)
    pl.semaphore_signal(barrier, inc=1, device_id=hop, device_id_type=MESH)

    @pl.when(jnp.logical_not(outer))
    def _():
        pl.semaphore_signal(barrier, inc=1, device_id=across, device_id_type=MESH)
        pl.semaphore_wait(barrier, m + 1)

    @pl.when(outer)
    def _():
        pl.semaphore_wait(barrier, m)

    def lanes(p):
        return pl.ds(pl.multiple_of(p * qd, qd), qd)

    def b_copy(slot, d):
        p = (q + d) % m
        return pltpu.make_async_remote_copy(
            src_ref=x_ref.at[(k * p + slot) % occ], dst_ref=bs.at[slot, :, lanes(q)],
            send_sem=b_send.at[slot, d - 1], recv_sem=b_recv.at[slot, d - 1],
            device_id={"aux": first + p}, device_id_type=MESH,
        )

    def b_own(slot):
        return pltpu.make_async_copy(
            x_ref.at[(k * q + slot) % occ], bs.at[slot, :, lanes(q)], b_local.at[slot]
        )

    def b_wait(slot):
        b_own(slot).wait()
        for d in range(1, m):
            p = (q + m - d) % m
            pltpu.make_async_remote_copy(
                src_ref=x_ref.at[0], dst_ref=bs.at[slot, :, lanes(p)],
                send_sem=b_send.at[slot, d - 1], recv_sem=b_recv.at[slot, d - 1],
                device_id={"aux": first + p}, device_id_type=MESH,
            ).wait_recv()

    def b_start(slot):
        b_own(slot).start()
        for d in range(1, m):
            b_copy(slot, d).start()

    b_start(k - 1)

    def piece(buf, unit, kind, c):
        a, b = strips[c]
        return buf.at[unit, a : min(b, nvr), (0 if kind else a) : nvp]

    def hop_copy(src, dst, send, recv, target, unit, kind, c):
        return pltpu.make_async_remote_copy(
            src_ref=piece(src, unit, kind, c), dst_ref=piece(dst, unit, kind, c),
            send_sem=send.at[unit, c], recv_sem=recv.at[unit, c],
            device_id=target, device_id_type=MESH,
        )

    def inward(unit, kind, c):
        return hop_copy(cbuf, rbuf, s12, r13, hop, unit, kind, c)

    def exchange(unit, kind, c):
        return hop_copy(cbuf, xbuf, s12, r2, across, unit, kind, c)

    def outward(unit, kind, c):
        return hop_copy(rbuf, rbuf, s3, r13, hop, unit, kind, c)

    def partial(r, kind, before, between):
        s = (r + k - 1) % k
        unit = 2 * r + kind
        for c, (a, b) in enumerate(strips):
            low = 0 if kind else a
            got = lax.dot_general(
                bs[s, a:b, :], bs[s + kind, low:nvp, :], (((1,), (1,)), ((), ())),
                preferred_element_type=F32,
            )
            cbuf[unit, a:b, low:nvp] = got.astype(BF16)

            @pl.when(outer)
            def _():
                @pl.when(unit > 0)
                def _():
                    earlier = jnp.maximum(2 * r - 2 * before[0], 0) + before[1]
                    inward(earlier, before[1], c).wait_send()

                inward(unit, kind, c).start()

        @pl.when(jnp.logical_not(outer))
        def _():
            for c in range(len(strips)):
                inward(unit, kind, c).wait_recv()
                mine, theirs = piece(cbuf, unit, kind, c), piece(rbuf, unit, kind, c)
                mine[...] = (mine[...].astype(F32) + theirs[...].astype(F32)).astype(BF16)
                exchange(unit, kind, c).start()
                if c == 0:
                    between()

    def energies(r, kind):
        s = (r + k - 1) % k
        i = (k * q + s) % occ
        j = (i + kind) % occ
        return occ_ref[i] + occ_ref[j], kept_ref[i] == 1

    def t_block(unit, e, a, b, c, d):
        coulomb = cbuf[unit, a:b, c:d].astype(F32) + xbuf[unit, a:b, c:d].astype(F32)
        return coulomb / (e - vcol_ref[a:b, :] - vrow_ref[:, c:d])

    def u_diag(r):
        unit = 2 * r
        e, _ = energies(r, 0)
        for c, (a, b) in enumerate(strips):
            b = min(b, nvr)
            exchange(unit, 0, c).wait_recv()
            rbuf[unit, a:b, a:nvp] = t_block(unit, e, a, b, a, nvp).astype(BF16)
            outward(unit, 0, c).start()

    def u_pair(r):
        unit = 2 * r + 1
        e, flag = energies(r, 1)
        for c in range(len(strips)):
            exchange(unit, 1, c).wait_recv()
        for c, (a, b) in enumerate(strips):
            for a2, b2 in strips[c:]:
                upper = t_block(unit, e, a, b, a2, b2)
                lower = upper if a2 == a else t_block(unit, e, a2, b2, a, b)
                u = jnp.where(flag, 2.0 * upper - lower.T, 0.0)
                rbuf[unit, a:b, a2:b2] = u.astype(BF16)
                if a2 != a:
                    u = jnp.where(flag, 2.0 * lower - upper.T, 0.0)
                    rbuf[unit, a2:b2, a:b] = u.astype(BF16)
            outward(unit, 1, c).start()

    def t_copy():
        return pltpu.make_async_remote_copy(
            src_ref=tt.at[0], dst_ref=tt.at[1], send_sem=t_send, recv_sem=t_recv,
            device_id={"aux": first + (q + 1) % m}, device_id_type=MESH,
        )

    def g_copy(s, d):
        p = (q + d) % m
        return pltpu.make_async_remote_copy(
            src_ref=gbuf.at[s, 0:nvr, lanes(p)], dst_ref=out_ref.at[k * q + s, 0:nvr, :],
            send_sem=g_send.at[s, d - 1], recv_sem=g_recv.at[s, d - 1],
            device_id={"aux": first + p}, device_id_type=MESH,
        )

    def g_own(s):
        return pltpu.make_async_copy(
            gbuf.at[s, 0:nvr, lanes(q)], out_ref.at[k * q + s, 0:nvr, :], g_local.at[s]
        )

    def diag_ready(r):
        unit = 2 * r

        @pl.when(outer)
        def _():
            for c in range(len(strips)):
                outward(unit, 0, c).wait_recv()

        for c, (a, b) in enumerate(strips):
            for a2, b2 in strips[c + 1 :]:
                mirrored = rbuf[unit, a:b, a2:b2].astype(F32).T
                rbuf[unit, a2:b2, a:b] = mirrored.astype(BF16)

    def pair_ready(r):
        @pl.when(outer)
        def _():
            for c in range(len(strips)):
                outward(2 * r + 1, 1, c).wait_recv()

    def gamma(s, diag, given):
        for a, b in wide:
            b = min(b, nvr)
            total = jnp.dot(rbuf[diag, a:b, :], bs[s], preferred_element_type=F32)
            total += jnp.dot(rbuf[diag + 1, a:b, :], bs[s + 1], preferred_element_type=F32)
            gbuf[s, a:b, :] = (total + tt[given, a:b, :].astype(F32)).astype(BF16)
        g_own(s).start()
        for d in range(1, m):
            g_copy(s, d).start()

    def to_next(r, where):
        s = (r + k - 1) % k
        for a, b in wide:
            got = lax.dot_general(
                rbuf[2 * r + 1, 0:nvr, a:b], bs[s, 0:nvr, :], (((0,), (0,)), ((), ())),
                preferred_element_type=F32,
            )
            tt[where, a:b, :] = got.astype(BF16)

    def density(r):
        last = r == k - 1

        @pl.when(last)
        def _():
            t_copy().wait_send()

        pair_ready(r)

        @pl.when(r < k - 1)
        def _():
            diag_ready(r)

        @pl.when(r == 1)
        def _():
            t_copy().wait_recv()

        @pl.when((r >= 1) & (r < k - 1))
        def _():
            gamma(r - 1, 2 * r, 1)

        to_next(r, jnp.where((r == 0) | last, 0, 1))

        @pl.when(last)
        def _():
            @pl.loop(0, 2)
            def _(turn):
                @pl.when(turn == 1)
                def _():
                    diag_ready(r)

                gamma(k - 1 - turn, 2 * r * turn, turn)

        @pl.when(r == 0)
        def _():
            t_copy().start()

    @pl.loop(0, k + 1)
    def _(r):
        s = (r + k - 1) % k

        @pl.when(r <= 1)
        def _():
            b_wait(s)

            @pl.when(r == 0)
            def _():
                b_start(k)

            @pl.when(2 * r < k - 1)
            def _():
                b_start(2 * r)

        def pair_before():
            @pl.when(r >= 1)
            def _():
                u_pair(r - 1)

        @pl.when(r < k - 1)
        def _():
            partial(r, 0, (1, 1), pair_before)
            b_wait(s + 1)
            later = jnp.where(r == 0, 1, r + 2)

            @pl.when(later < k - 1)
            def _():
                b_start(later)

            partial(r, 1, (0, 0), lambda: u_diag(r))

        @pl.when(r == k - 1)
        def _():
            partial(r, 1, (1, 1), pair_before)
            partial(r, 0, (0, 1), lambda: u_pair(r))

            @pl.when(jnp.logical_not(outer))
            def _():
                u_diag(r)

        @pl.when(r >= 1)
        def _():
            density(r - 1)

    @pl.loop(0, k + 1)
    def _(slot):
        for d in range(1, m):
            b_copy(slot, d).wait_send()

    @pl.loop(0, k)
    def _(s):
        @pl.when(outer & (s == k - 1))
        def _():
            for c in range(len(strips)):
                inward(2 * s, 0, c).wait_send()

        @pl.when(jnp.logical_not(outer))
        def _():
            for kind in (0, 1):
                for c in range(len(strips)):
                    exchange(2 * s + kind, kind, c).wait_send()
                    outward(2 * s + kind, kind, c).wait_send()

        g_own(s).wait()
        for d in range(1, m):
            g_copy(s, d).wait_send()
            p = (q + m - d) % m
            pltpu.make_async_remote_copy(
                src_ref=gbuf.at[s, 0:nvr, lanes(p)], dst_ref=out_ref.at[k * p + s, 0:nvr, :],
                send_sem=g_send.at[s, d - 1], recv_sem=g_recv.at[s, d - 1],
                device_id={"aux": first + p}, device_id_type=MESH,
            ).wait_recv()


def body(b_factors, occ_energy, vir_energy, kept):
    occ, nv, qd = b_factors.shape
    m = lax.axis_size("aux") // PLANES
    k = occ // m
    nvp, nvr = up_to(nv, 128), up_to(nv, 16)
    x = jnp.pad(b_factors, ((0, 0), (0, nvp - nv), (0, 0)))
    vir = jnp.pad(vir_energy, (0, nvp - nv), constant_values=1.0)
    pieces = len(range(0, nvp, STRIP))
    square = pltpu.VMEM((2 * k, nvp, nvp), BF16)
    dma = pltpu.SemaphoreType.DMA
    flops = 2 * nvp * nvp * m * qd * 5 * k
    out = pl.pallas_call(
        functools.partial(kernel, m, k),
        out_shape=jax.ShapeDtypeStruct((occ, nvr, qd), BF16),
        in_specs=[pl.BlockSpec(memory_space=pltpu.SMEM)] * 2
        + [pl.BlockSpec(memory_space=pltpu.VMEM)] * 2
        + [pl.BlockSpec(memory_space=pl.ANY)],
        out_specs=pl.BlockSpec(memory_space=pl.ANY),
        scratch_shapes=[
            pltpu.VMEM((k + 1, nvp, m * qd), BF16), square, square, square,
            pltpu.VMEM((2, nvp, m * qd), BF16), pltpu.VMEM((k, nvp, m * qd), BF16),
            dma((k + 1, m - 1)), dma((k + 1, m - 1)), dma((k + 1,)),
            dma((2 * k, pieces)), dma((2 * k, pieces)), dma((2 * k, pieces)), dma((2 * k, pieces)),
            dma, dma, dma((k, m - 1)), dma((k, m - 1)), dma((k,)),
        ],
        compiler_params=pltpu.CompilerParams(
            collective_id=0, has_side_effects=True, vmem_limit_bytes=63 * 2**20
        ),
        cost_estimate=pl.CostEstimate(flops=flops, bytes_accessed=4 * x.size, transcendentals=0),
    )(occ_energy, kept, vir[None, :], vir[:, None], x)
    return out[:, :nv]


def solution(mesh):
    placed = (P("groups", None, "aux"), P("groups"), P("groups"), P("groups"))
    return jax.shard_map(
        body, mesh=mesh, in_specs=placed, out_specs=P("groups", None, "aux"), check_vma=False
    )
```
